32 devices in a mesh: groups: 2 (over x), ep: 16 (over z, y, core).
Axes of the slice: x: 2, y: 2, z: 4, core: 2. Of those that a mesh axis runs over, the one named last changes fastest.
Arguments:
- residual: bfloat16 [512, 2048], P(('groups', 'ep')), parts along dimension 0, may hold values from -54 to 54
- norm_gain: bfloat16 [2048], replicated, may hold values from 0.099609375 to 1.8984375
- expert_ids: int32 [512, 8], P(('groups', 'ep')), parts along dimension 0, may hold values from 0 to 15, as said below
- route_weights: float32 [512, 8], P(('groups', 'ep')), parts along dimension 0, may hold values from 0.05 to 1
- w_gate: bfloat16 [16, 2, 2048, 384], P('ep'), may hold values from -0.125 to 0.125
- w_up: bfloat16 [16, 2, 2048, 384], P('ep'), may hold values from -0.125 to 0.125
- w_down: bfloat16 [16, 2, 384, 2048], P('ep'), may hold values from -0.21875 to 0.21875
Outputs:
- layer_out: bfloat16 [512, 2048], P(('groups', 'ep')), parts along dimension 0
The draws below stay inside these ranges and needn't reach their ends.
There are 2 independent parts, one for each index of `groups`. The reference program is written for one: setup_inputs(seed, part) draws one part's arguments, and reference() takes and returns one part's arrays. A program takes and returns all parts, laid end to end along the dimension named above; an argument that names none is the same for every part. Nothing has to cross between parts.
Inputs may be any that keep to these rules, and one draw needn't show every extreme that they name: `expert_ids`: each row names 8 different experts. Among the rows of one device no expert is named by more than 16 rows, and no pair of experts 2 j and 2 j + 1 by more than 16 rows (a row that names both counts once); each bound is reached on some device.
All inputs are finite; a program needn't handle non-finite values.
Results may differ from the reference program's by a relative error of at most 0.004.
Values may be sent and summed in bfloat16 or wider, within the bound.
A program may use at most 64 MiB of HBM per device.

```python
import math
import jax
import jax.numpy as jnp
from jax import lax

D = 2048
FF = 768
TOP = 8
REQ_DEV = 16
EXPERTS = 16
REQ = 256
CAP = 16
BCAP = 16
N_EP = 16


def draw_residual(key, part):
    values = jax.random.truncated_normal(jax.random.fold_in(key, 31), -6.0, 6.0, (REQ, D), jnp.float32)
    return values.astype(jnp.bfloat16)


def draw_expert_ids(key, part):
    block_total = EXPERTS // 2
    ranking = jax.random.permutation(jax.random.fold_in(key, 21), EXPERTS).astype(jnp.int32)
    standing = jnp.zeros((EXPERTS,), jnp.int32).at[ranking].set(jnp.arange(EXPERTS, dtype=jnp.int32))
    frequent_experts = 24 * (standing < max(1, EXPERTS // 8)).astype(jnp.int32) + 24 * (standing < max(1, EXPERTS // 32)).astype(jnp.int32)
    heaviest_expert = ranking[0]
    offset_block = jax.random.randint(jax.random.fold_in(key, 22), (), 1, block_total)
    last_block = block_total - 1
    planted = jnp.where(heaviest_expert // 2 == last_block, (heaviest_expert // 2 + offset_block) % block_total, last_block).astype(jnp.int32)
    random_noise = jax.random.randint(jax.random.fold_in(key, 23), (N_EP, REQ_DEV, EXPERTS), 0, 64)
    expert_pool = jnp.arange(EXPERTS, dtype=jnp.int32)
    row_index = jnp.arange(REQ_DEV, dtype=jnp.int32)
    favored_expert_boost = jnp.where(expert_pool == heaviest_expert, 1000, 0)
    inserted_choice = 2 * planted + row_index % 2
    inserted_expert_boost = jnp.where(expert_pool[None, :] == inserted_choice[:, None], 900, 0)
    router_logits = random_noise + frequent_experts[None, None, :] + favored_expert_boost[None, None, :] + inserted_expert_boost[None, :, :]
    ordered = (router_logits * EXPERTS + expert_pool[None, None, :]).astype(jnp.int32)

    def one_device(device_scores):

        def one_row(carry_state, row_scores):
            counts, block_counts = carry_state
            allowed = jnp.logical_and(counts < CAP, jnp.repeat(block_counts, 2) < BCAP)
            masked = jnp.where(allowed, row_scores, -1)
            chosen = lax.top_k(masked, TOP)[1].astype(jnp.int32)
            onehot = (chosen[:, None] == expert_pool[None, :]).astype(jnp.int32)
            taken_now = jnp.sum(onehot, axis=0)
            counts = counts + taken_now
            block_counts = block_counts + (jnp.sum(taken_now.reshape(block_total, 2), axis=1) > 0).astype(jnp.int32)
            return ((counts, block_counts), chosen)
        start_state = (jnp.zeros((EXPERTS,), jnp.int32), jnp.zeros((block_total,), jnp.int32))
        return lax.scan(one_row, start_state, device_scores)[1]
    routes = jax.vmap(one_device)(ordered)
    return routes.reshape(REQ, TOP).astype(jnp.int32)


def levels(stream_key, dims, shards, smallest, largest):
    loudness, own = 1.0, jax.random.fold_in(stream_key, 6)
    for position, shards_of in shards:
        steps = jnp.exp(jax.random.uniform(jax.random.fold_in(own, position), (shards_of,), jnp.float32, smallest / len(shards), largest / len(shards)))
        loudness = loudness * jnp.repeat(steps, dims[position] // shards_of).reshape([-1 if axis == position else 1 for axis in range(len(dims))])
    return loudness


def normal_values(own_key, shape, spread, reach, split=(), kind=jnp.bfloat16):
    factor_of = levels(own_key, shape, split, -0.22, 0.18) if split else 1.0
    values = jax.random.normal(own_key, shape, jnp.float32) * spread * factor_of
    return jnp.minimum(jnp.maximum(values, -reach), reach).astype(kind)


def setup_inputs(seed: int = 0, part: int = 0) -> dict:
    streams_of = jax.random.split(jax.random.key(seed), 8)
    part_splits = jax.random.split(jax.random.fold_in(streams_of[7], part), 8)
    return {
        "residual": draw_residual(jax.random.fold_in(jax.random.fold_in(streams_of[7], part), 71), part),
        "norm_gain": jnp.clip(1.0 + 0.18 * jax.random.normal(streams_of[1], (D,), jnp.float32), 0.099609375, 1.8984375).astype(jnp.bfloat16),
        "expert_ids": draw_expert_ids(jax.random.fold_in(jax.random.fold_in(streams_of[7], part), 71), part),
        "route_weights": jnp.clip(jnp.exp(math.log(1.0) - 2.9957323 * jax.random.uniform(part_splits[3], (REQ, TOP), jnp.float32) ** levels(part_splits[3], (REQ, TOP), ((0, 16),), -0.2, 0.2)), 0.05, 1.0),
        "w_gate": normal_values(streams_of[4], (EXPERTS, 2, D, FF // 2), D ** -0.5, 0.125, ((0, 16),)),
        "w_up": normal_values(streams_of[5], (EXPERTS, 2, D, FF // 2), D ** -0.5, 0.125, ((0, 16),)),
        "w_down": normal_values(streams_of[6], (EXPERTS, 2, FF // 2, D), FF ** -0.5, 0.21875, ((0, 16),)),
    }


def reference(residual, norm_gain, expert_ids, route_weights, w_gate, w_up, w_down):
    widened = residual.astype(jnp.float32)
    scaling = lax.rsqrt(lax.optimization_barrier(jnp.mean(widened * widened, axis=1, keepdims=True)) + 1e-06)
    normed = (widened * scaling * norm_gain.astype(jnp.float32)[None, :]).astype(jnp.bfloat16)
    shares = (route_weights / lax.optimization_barrier(jnp.sum(route_weights, axis=1, keepdims=True))).astype(jnp.bfloat16)
    flat_ids = expert_ids.reshape(-1)
    flat_shares = shares.reshape(-1).astype(jnp.float32)
    row_count = residual.shape[0]
    bound_rows = N_EP * CAP

    def one_expert(combined, expert_index):
        chosen = flat_ids == expert_index
        picked = jnp.nonzero(chosen, size=bound_rows, fill_value=0)[0].astype(jnp.int32)
        filled = jnp.arange(bound_rows, dtype=jnp.int32) < jnp.sum(chosen.astype(jnp.int32))
        selected = normed[picked // TOP]
        first_slot = 2 * (expert_index // 2)
        member = expert_index % 2
        gate_mat = jnp.concatenate([w_gate[first_slot, member], w_gate[first_slot + 1, member]], axis=1)
        up_mat = jnp.concatenate([w_up[first_slot, member], w_up[first_slot + 1, member]], axis=1)
        down_mat = jnp.concatenate([w_down[first_slot, member], w_down[first_slot + 1, member]], axis=0)
        gate_part = jnp.dot(selected, gate_mat, preferred_element_type=jnp.float32)
        upper = jnp.dot(selected, up_mat, preferred_element_type=jnp.float32)
        inner = (jax.nn.silu(gate_part) * upper).astype(jnp.bfloat16)
        answer = jnp.dot(inner, down_mat, preferred_element_type=jnp.float32)
        weight = jnp.where(filled, flat_shares[picked], jnp.zeros((), jnp.float32))
        targets = jnp.where(filled, picked // TOP, row_count)
        return (combined.at[targets].add(weight[:, None] * answer, mode='drop'), expert_index)
    combined = lax.scan(one_expert, jnp.zeros((row_count, D), jnp.float32), jnp.arange(EXPERTS, dtype=jnp.int32))[0]
    return (widened + combined).astype(jnp.bfloat16)
```

```python
import functools

import jax
import jax.numpy as jnp
from jax import lax
from jax.experimental import pallas as pl
from jax.experimental.pallas import tpu as pltpu
from jax.sharding import PartitionSpec as P

TOP = 8


def swapped(value, axis, distance):
    mask = 2**distance
    pairs = [(source, source ^ mask) for source in range(lax.axis_size(axis))]
    return lax.ppermute(value, axis, pairs)


def half_ffn(inputs, gate_mat, up_mat, down_mat):
    gate_part = jnp.dot(inputs, gate_mat, preferred_element_type=jnp.float32)
    upper = jnp.dot(inputs, up_mat, preferred_element_type=jnp.float32)
    inner = (jax.nn.silu(gate_part) * upper).astype(jnp.bfloat16)
    return jnp.dot(inner, down_mat, preferred_element_type=jnp.float32)


def pair_tables(expert_ids, shares, normed, block_total, slot_total):
    local_rows = normed.shape[0]
    expert_total = 2 * block_total
    block_iota = lax.broadcasted_iota(jnp.int32, (1, 1, block_total), 2)
    block_hits = jnp.any((expert_ids // 2)[:, :, None] == block_iota, axis=1).astype(jnp.int32)
    block_rank = jnp.cumsum(block_hits, axis=0) - 1
    hit_wide = jnp.repeat(block_hits, slot_total, axis=1)
    rank_wide = jnp.repeat(block_rank, slot_total, axis=1)
    slot_place = lax.broadcasted_iota(jnp.int32, (1, block_total * slot_total), 1) % slot_total
    picker = jnp.logical_and(hit_wide > 0, rank_wide == slot_place)
    expert_iota = lax.broadcasted_iota(jnp.int32, (1, 1, expert_total), 2)
    expert_mask = expert_ids[:, :, None] == expert_iota
    share_table = jnp.sum(
        jnp.where(expert_mask, shares[:, :, None], jnp.zeros((), jnp.bfloat16)), axis=1
    )
    share_wide = jnp.repeat(share_table.reshape(local_rows, block_total, 2), slot_total, axis=1)
    slot_weights = jnp.sum(
        jnp.where(picker[:, :, None], share_wide, jnp.zeros((), jnp.bfloat16)), axis=0
    )
    slot_rows = jnp.einsum(
        "rs,rd->sd", picker.astype(jnp.bfloat16), normed, preferred_element_type=jnp.float32
    ).astype(jnp.bfloat16)
    return (picker, slot_rows, slot_weights)


LANES = 128


def mixture_kernel(
    depth,
    residual_ref,
    gain_ref,
    ids_ref,
    weights_ref,
    gate_hbm,
    up_hbm,
    down_hbm,
    out_ref,
    first_mats,
    down_mats,
    rows,
    kept,
    core_out,
    core_in,
    y_out,
    y_in,
    z_out,
    z_in,
    weight_sems,
    rows_recv,
    rows_z_send,
    rows_y_send,
    rows_core_send,
    core_send,
    core_recv,
    y_send,
    y_recv,
    z_send,
    z_recv,
):
    place = lax.axis_index("ep")
    core = place % 2
    chip = place // 2
    y_at = chip % 2
    z_at = chip // 2
    mate = place + 1 - 2 * core
    y_peer = place + 2 - 4 * y_at

    def z_peer(step):
        return ((z_at + step) % depth) * 4 + y_at * 2 + core

    local_rows, width = residual_ref.shape
    half = gate_hbm.shape[3]
    hidden = 2 * half

    loads = []
    for member in range(2):
        for which, source in enumerate((gate_hbm, up_hbm)):
            loads.append(
                pltpu.make_async_copy(
                    source.at[0, member],
                    first_mats.at[:, pl.ds(which * hidden + member * half, half)],
                    weight_sems.at[2 * member + which],
                )
            )
    for member in range(2):
        loads.append(
            pltpu.make_async_copy(
                down_hbm.at[0, member],
                down_mats.at[pl.ds(member * half, half), :],
                weight_sems.at[4 + member],
            )
        )
    for load in loads:
        load.start()

    barrier = pltpu.get_barrier_semaphore()
    for peer in [mate, y_peer] + [z_peer(step) for step in range(1, depth)]:
        pl.semaphore_signal(
            barrier, inc=1, device_id={"ep": peer}, device_id_type=pl.DeviceIdType.MESH
        )

    widened = residual_ref[...].astype(jnp.float32)
    scaling = lax.rsqrt(jnp.mean(widened * widened, axis=1, keepdims=True) + 1e-06)
    gain = gain_ref[...].astype(jnp.float32)
    rows[0, 0, 0, :, 0:width] = (widened * scaling * gain).astype(jnp.bfloat16)
    route = weights_ref[...]
    shares = (route / jnp.sum(route, axis=1, keepdims=True)).astype(jnp.bfloat16).astype(jnp.float32)
    ids = ids_ref[...]
    lane = lax.broadcasted_iota(jnp.int32, (local_rows, LANES), 1)
    table = jnp.zeros((local_rows, LANES), jnp.float32)
    for choice in range(ids.shape[1]):
        table = table + jnp.where(
            ids[:, choice : choice + 1] == lane, shares[:, choice : choice + 1], 0.0
        )
    rows[0, 0, 0, :, width : width + LANES] = table.astype(jnp.bfloat16)

    pl.semaphore_wait(barrier, depth + 1)

    started = []

    def send(source, target, send_sem, recv_sem, peer):
        copy = pltpu.make_async_remote_copy(
            src_ref=source,
            dst_ref=target,
            send_sem=send_sem,
            recv_sem=recv_sem,
            device_id={"ep": peer},
            device_id_type=pl.DeviceIdType.MESH,
        )
        copy.start()
        started.append(copy)
        return copy

    def arrived(step, dy, dc):
        slot = rows.at[step, dy, dc]
        pltpu.make_async_copy(slot, slot, rows_recv.at[step, dy, dc]).wait()

    def landed(buffer, sem):
        pltpu.make_async_copy(buffer, buffer, sem).wait()

    def rows_to_z(step):
        send(
            rows.at[0, 0, 0],
            rows.at[step, 0, 0],
            rows_z_send.at[step],
            rows_recv.at[step, 0, 0],
            z_peer(step),
        )

    def rows_to_y(step):
        send(
            rows.at[step, 0, 0],
            rows.at[step, 1, 0],
            rows_y_send.at[step],
            rows_recv.at[step, 1, 0],
            y_peer,
        )

    def rows_to_mate(step, dy):
        send(
            rows.at[step, dy, 0],
            rows.at[step, dy, 1],
            rows_core_send.at[step, dy],
            rows_recv.at[step, dy, 1],
            mate,
        )

    def from_z(step):
        arrived(step, 0, 0)
        rows_to_y(step)
        rows_to_mate(step, 0)

    def from_y(step):
        arrived(step, 1, 0)
        rows_to_mate(step, 1)

    def compute(step):
        arrived(step, 0, 1)
        arrived(step, 1, 1)
        block = rows[step, :, :, :, 0:width].reshape(4 * local_rows, width)
        shares_here = rows[step, :, :, :, width : width + LANES].reshape(4 * local_rows, LANES)
        shares_here = shares_here.astype(jnp.float32)
        lanes = lax.broadcasted_iota(jnp.int32, (4 * local_rows, LANES), 1)
        both = jnp.dot(block, first_mats[...], preferred_element_type=jnp.float32)
        parts = []
        for member in range(2):
            share = jnp.sum(
                jnp.where(lanes == 2 * chip + member, shares_here, 0.0), axis=1, keepdims=True
            )
            gate_part = both[:, member * half : (member + 1) * half]
            upper = both[:, hidden + member * half : hidden + (member + 1) * half]
            inner = (jax.nn.silu(gate_part) * upper).astype(jnp.bfloat16)
            parts.append((inner.astype(jnp.float32) * share).astype(jnp.bfloat16))
        inner = jnp.concatenate(parts, axis=1)
        answer = jnp.dot(inner, down_mats[...], preferred_element_type=jnp.float32)
        answer = answer.reshape(2, 2, local_rows, width)
        kept[step] = answer[:, 0]
        core_out[step] = answer[:, 1].astype(jnp.bfloat16)
        send(core_out.at[step], core_in.at[step], core_send.at[step], core_recv.at[step], mate)

    def add_core(step):
        landed(core_in.at[step], core_recv.at[step])
        y_out[step] = (kept[step, 1] + core_in[step, 1].astype(jnp.float32)).astype(jnp.bfloat16)
        send(y_out.at[step], y_in.at[step], y_send.at[step], y_recv.at[step], y_peer)
        kept[step, 0] = kept[step, 0] + core_in[step, 0].astype(jnp.float32)

    def add_y(step):
        landed(y_in.at[step], y_recv.at[step])
        total = kept[step, 0] + y_in[step].astype(jnp.float32)
        if step == 0:
            kept[0, 0] = total
        else:
            z_out[step] = total.astype(jnp.bfloat16)
            send(
                z_out.at[step],
                z_in.at[step],
                z_send.at[step],
                z_recv.at[step],
                z_peer(depth - step),
            )

    for step in range(1, depth):
        rows_to_z(step)
    rows_to_y(0)
    rows_to_mate(0, 0)
    from_y(0)
    if depth > 1:
        from_z(1)
    for load in loads:
        load.wait()
    for step in range(depth):
        compute(step)
        if step + 2 < depth:
            from_z(step + 2)
        if step + 1 < depth:
            from_y(step + 1)
        if step >= 1:
            add_core(step - 1)
        if step >= 2:
            add_y(step - 2)
    add_core(depth - 1)
    if depth > 1:
        add_y(depth - 2)
    add_y(depth - 1)

    total = residual_ref[...].astype(jnp.float32) + kept[0, 0]
    for step in range(1, depth):
        landed(z_in.at[step], z_recv.at[step])
        total = total + z_in[step].astype(jnp.float32)
    out_ref[...] = total.astype(out_ref.dtype)
    for copy in started:
        copy.wait_send()


def dense_mixture(residual, norm_gain, expert_ids, route_weights, w_gate, w_up, w_down):
    local_rows, width = residual.shape
    half = w_gate.shape[3]
    device_total = lax.axis_size("ep")
    depth = device_total // 4
    dma = pltpu.SemaphoreType.DMA
    bf16 = jnp.bfloat16
    vmem = pl.BlockSpec(memory_space=pltpu.VMEM)
    anywhere = pl.BlockSpec(memory_space=pl.ANY)
    flops = 2 * device_total * local_rows * width * half * 6
    return pl.pallas_call(
        functools.partial(mixture_kernel, depth),
        out_shape=jax.ShapeDtypeStruct(residual.shape, residual.dtype),
        in_specs=[vmem] * 4 + [anywhere] * 3,
        out_specs=vmem,
        scratch_shapes=[
            pltpu.VMEM((width, 4 * half), bf16),
            pltpu.VMEM((2 * half, width), bf16),
            pltpu.VMEM((depth, 2, 2, local_rows, width + LANES), bf16),
            pltpu.VMEM((depth, 2, local_rows, width), jnp.float32),
            pltpu.VMEM((depth, 2, local_rows, width), bf16),
            pltpu.VMEM((depth, 2, local_rows, width), bf16),
            pltpu.VMEM((depth, local_rows, width), bf16),
            pltpu.VMEM((depth, local_rows, width), bf16),
            pltpu.VMEM((depth, local_rows, width), bf16),
            pltpu.VMEM((depth, local_rows, width), bf16),
            dma((6,)),
            dma((depth, 2, 2)),
            dma((depth,)),
            dma((depth,)),
            dma((depth, 2)),
            dma((depth,)),
            dma((depth,)),
            dma((depth,)),
            dma((depth,)),
            dma((depth,)),
            dma((depth,)),
        ],
        compiler_params=pltpu.CompilerParams(
            collective_id=0, has_side_effects=True, vmem_limit_bytes=62 * 2**20
        ),
        cost_estimate=pl.CostEstimate(
            flops=flops, bytes_accessed=12 * width * half, transcendentals=0
        ),
    )(residual, norm_gain[None, :], expert_ids, route_weights, w_gate, w_up, w_down)


def local(residual, norm_gain, expert_ids, route_weights, w_gate, w_up, w_down):
    local_rows = residual.shape[0]
    model_width = residual.shape[1]
    device_total = lax.axis_size("ep")
    block_total = device_total // 2
    typical = max(1, local_rows * TOP // device_total)
    pair_slots = min(local_rows, 4 * typical)
    if pair_slots == local_rows and device_total % 4 == 0 and device_total <= LANES:
        return dense_mixture(
            residual, norm_gain, expert_ids, route_weights, w_gate, w_up, w_down
        )
    widened = residual.astype(jnp.float32)
    scaling = lax.rsqrt(jnp.mean(widened * widened, axis=1, keepdims=True) + 1e-06)
    normed = (widened * scaling * norm_gain.astype(jnp.float32)[None, :]).astype(jnp.bfloat16)
    shares = (route_weights / jnp.sum(route_weights, axis=1, keepdims=True)).astype(jnp.bfloat16)

    def weighted_both(arrived, arrived_weights):
        flat_rows = arrived.reshape(-1, arrived.shape[2])
        flat_weights = arrived_weights.reshape(-1, 2).astype(jnp.float32)
        mixed = flat_weights[:, 0:1] * half_ffn(flat_rows, w_gate[0, 0], w_up[0, 0], w_down[0, 0])
        mixed = mixed + flat_weights[:, 1:2] * half_ffn(
            flat_rows, w_gate[0, 1], w_up[0, 1], w_down[0, 1]
        )
        return mixed.reshape(arrived.shape)

    half_slots = (pair_slots + 1) // 2
    padded_slots = 2 * half_slots
    picker, slot_rows, slot_weights = pair_tables(
        expert_ids, shares, normed, block_total, padded_slots
    )
    outgoing = slot_rows.reshape(device_total, half_slots, model_width)
    weights_out = slot_weights.reshape(device_total, half_slots, 2)
    arrived = lax.all_to_all(outgoing, "ep", split_axis=0, concat_axis=0, tiled=True)
    arrived_weights = lax.all_to_all(weights_out, "ep", split_axis=0, concat_axis=0, tiled=True)
    other_rows, other_weights = swapped((arrived, arrived_weights), "ep", 0)
    mine = weighted_both(arrived, arrived_weights)
    theirs = weighted_both(other_rows, other_weights)
    back = swapped(theirs, "ep", 0)
    answered = mine + back
    returned = lax.all_to_all(answered, "ep", split_axis=0, concat_axis=0, tiled=True)
    pooled = returned.reshape(block_total * padded_slots, model_width)
    combined = jnp.dot(picker.astype(jnp.float32), pooled, precision=lax.Precision.HIGHEST)
    return (widened + combined).astype(jnp.bfloat16)


def solution(mesh):
    placed = (
        P(("groups", "ep"), None),
        P(),
        P(("groups", "ep"), None),
        P(("groups", "ep"), None),
        P("ep", None, None, None),
        P("ep", None, None, None),
        P("ep", None, None, None),
    )
    return jax.shard_map(
        local, mesh=mesh, in_specs=placed, out_specs=P(("groups", "ep"), None), check_vma=False
    )
```

```python
import functools

import jax
import jax.numpy as jnp
from jax import lax
from jax.experimental import pallas as pl
from jax.experimental.pallas import tpu as pltpu
from jax.sharding import PartitionSpec as P

TOP = 8


def swapped(value, axis, distance):
    mask = 2**distance
    pairs = [(source, source ^ mask) for source in range(lax.axis_size(axis))]
    return lax.ppermute(value, axis, pairs)


def half_ffn(inputs, gate_mat, up_mat, down_mat):
    gate_part = jnp.dot(inputs, gate_mat, preferred_element_type=jnp.float32)
    upper = jnp.dot(inputs, up_mat, preferred_element_type=jnp.float32)
    inner = (jax.nn.silu(gate_part) * upper).astype(jnp.bfloat16)
    return jnp.dot(inner, down_mat, preferred_element_type=jnp.float32)


def pair_tables(expert_ids, shares, normed, block_total, slot_total):
    local_rows = normed.shape[0]
    expert_total = 2 * block_total
    block_iota = lax.broadcasted_iota(jnp.int32, (1, 1, block_total), 2)
    block_hits = jnp.any((expert_ids // 2)[:, :, None] == block_iota, axis=1).astype(jnp.int32)
    block_rank = jnp.cumsum(block_hits, axis=0) - 1
    hit_wide = jnp.repeat(block_hits, slot_total, axis=1)
    rank_wide = jnp.repeat(block_rank, slot_total, axis=1)
    slot_place = lax.broadcasted_iota(jnp.int32, (1, block_total * slot_total), 1) % slot_total
    picker = jnp.logical_and(hit_wide > 0, rank_wide == slot_place)
    expert_iota = lax.broadcasted_iota(jnp.int32, (1, 1, expert_total), 2)
    expert_mask = expert_ids[:, :, None] == expert_iota
    share_table = jnp.sum(
        jnp.where(expert_mask, shares[:, :, None], jnp.zeros((), jnp.bfloat16)), axis=1
    )
    share_wide = jnp.repeat(share_table.reshape(local_rows, block_total, 2), slot_total, axis=1)
    slot_weights = jnp.sum(
        jnp.where(picker[:, :, None], share_wide, jnp.zeros((), jnp.bfloat16)), axis=0
    )
    slot_rows = jnp.einsum(
        "rs,rd->sd", picker.astype(jnp.bfloat16), normed, preferred_element_type=jnp.float32
    ).astype(jnp.bfloat16)
    return (picker, slot_rows, slot_weights)


LANES = 128


def mixture_kernel(
    depth,
    groups,
    parts,
    residual_hbm,
    gain_hbm,
    ids_hbm,
    weights_hbm,
    gate_hbm,
    up_hbm,
    down_hbm,
    out_ref,
    residual_ref,
    gain_ref,
    ids_ref,
    weights_ref,
    first_mats,
    down_mats,
    rows,
    inner_ref,
    kept,
    core_out,
    core_in,
    y_out,
    y_in,
    z_out,
    z_in,
    small_sems,
    weight_sems,
    rows_recv,
    rows_z_send,
    rows_y_send,
    rows_core_send,
    core_send,
    core_recv,
    y_send,
    y_recv,
    z_send,
    z_recv,
):
    place = lax.axis_index("ep")
    core = place % 2
    chip = place // 2
    y_at = chip % 2
    z_at = chip // 2
    mate = place + 1 - 2 * core
    y_peer = place + 2 - 4 * y_at

    def z_peer(step):
        return ((z_at + step) % depth) * 4 + y_at * 2 + core

    local_rows, width = residual_ref.shape
    part_width = width // parts
    half = gate_hbm.shape[3]
    hidden = 2 * half

    smalls = []
    for which, (source, target) in enumerate(
        (
            (residual_hbm, residual_ref),
            (gain_hbm, gain_ref),
            (ids_hbm, ids_ref),
            (weights_hbm, weights_ref),
        )
    ):
        smalls.append(pltpu.make_async_copy(source, target, small_sems.at[which]))
    for load in smalls:
        load.start()

    barrier = pltpu.get_barrier_semaphore()
    for peer in [mate, y_peer] + [z_peer(step) for step in range(1, depth)]:
        pl.semaphore_signal(
            barrier, inc=1, device_id={"ep": peer}, device_id_type=pl.DeviceIdType.MESH
        )

    loads = []
    for member in range(2):
        for which, source in enumerate((gate_hbm, up_hbm)):
            loads.append(
                pltpu.make_async_copy(
                    source.at[0, member],
                    first_mats.at[:, pl.ds(which * hidden + member * half, half)],
                    weight_sems.at[2 * member + which],
                )
            )
    for member in range(2):
        loads.append(
            pltpu.make_async_copy(
                down_hbm.at[0, member],
                down_mats.at[pl.ds(member * half, half), :],
                weight_sems.at[4 + member],
            )
        )
    for load in smalls:
        load.wait()
    for load in loads:
        load.start()

    widened = residual_ref[...].astype(jnp.float32)
    scaling = lax.rsqrt(jnp.mean(widened * widened, axis=1, keepdims=True) + 1e-06)
    for block in range(width // LANES):
        columns = slice(block * LANES, (block + 1) * LANES)
        gain = gain_ref[block : block + 1, :].astype(jnp.float32)
        rows[0, 0, 0, :, columns] = (widened[:, columns] * scaling * gain).astype(jnp.bfloat16)
    route = weights_ref[...]
    shares = (route / jnp.sum(route, axis=0, keepdims=True)).astype(jnp.bfloat16).astype(jnp.float32)
    ids = ids_ref[...]
    expert = lax.broadcasted_iota(jnp.int32, (LANES, local_rows), 0)
    table = jnp.zeros((LANES, local_rows), jnp.float32)
    for choice in range(ids.shape[0]):
        table = table + jnp.where(
            ids[choice : choice + 1, :] == expert, shares[choice : choice + 1, :], 0.0
        )
    same = lax.broadcasted_iota(jnp.int32, (local_rows, local_rows), 0) == (
        lax.broadcasted_iota(jnp.int32, (local_rows, local_rows), 1)
    )
    turned = lax.dot_general(
        same.astype(jnp.float32).astype(jnp.bfloat16),
        table.astype(jnp.bfloat16),
        (((1,), (1,)), ((), ())),
        preferred_element_type=jnp.float32,
    )
    rows[0, 0, 0, :, width : width + LANES] = turned.astype(jnp.bfloat16)

    pl.semaphore_wait(barrier, depth + 1)

    started = []

    def send(source, target, send_sem, recv_sem, peer):
        copy = pltpu.make_async_remote_copy(
            src_ref=source,
            dst_ref=target,
            send_sem=send_sem,
            recv_sem=recv_sem,
            device_id={"ep": peer},
            device_id_type=pl.DeviceIdType.MESH,
        )
        copy.start()
        started.append(copy)

    def landed(buffer, sem):
        pltpu.make_async_copy(buffer, buffer, sem).wait()

    def arrived(step, dy, dc):
        landed(rows.at[step, dy, dc], rows_recv.at[step, dy, dc])

    def rows_to_z(step):
        send(
            rows.at[0, 0, 0],
            rows.at[step, 0, 0],
            rows_z_send.at[step],
            rows_recv.at[step, 0, 0],
            z_peer(step),
        )

    def rows_to_y(step):
        send(
            rows.at[step, 0, 0],
            rows.at[step, 1, 0],
            rows_y_send.at[step],
            rows_recv.at[step, 1, 0],
            y_peer,
        )

    def rows_to_mate(step, dy):
        send(
            rows.at[step, dy, 0],
            rows.at[step, dy, 1],
            rows_core_send.at[step, dy],
            rows_recv.at[step, dy, 1],
            mate,
        )

    def from_z(step):
        if 0 < step < depth:
            arrived(step, 0, 0)
            rows_to_y(step)
            rows_to_mate(step, 0)

    def from_y(step):
        if step < depth:
            arrived(step, 1, 0)
            rows_to_mate(step, 1)

    def first(group):
        begin, count = groups[group]
        for step in range(begin, begin + count):
            arrived(step, 0, 1)
            arrived(step, 1, 1)
        total_rows = count * 4 * local_rows
        block = rows[begin : begin + count, :, :, :, 0:width].reshape(total_rows, width)
        shares_here = rows[begin : begin + count, :, :, :, width : width + LANES]
        shares_here = shares_here.reshape(total_rows, LANES).astype(jnp.float32)
        lanes = lax.broadcasted_iota(jnp.int32, (total_rows, LANES), 1)
        both = jnp.dot(block, first_mats[...], preferred_element_type=jnp.float32)
        for member in range(2):
            share = jnp.sum(
                jnp.where(lanes == 2 * chip + member, shares_here, 0.0), axis=1, keepdims=True
            )
            gate_part = both[:, member * half : (member + 1) * half]
            upper = both[:, hidden + member * half : hidden + (member + 1) * half]
            inner = (jax.nn.silu(gate_part) * upper).astype(jnp.bfloat16)
            inner_ref[0:total_rows, member * half : (member + 1) * half] = (
                inner.astype(jnp.float32) * share
            ).astype(jnp.bfloat16)

    def down(group):
        begin, count = groups[group]
        steps = pl.ds(begin, count)
        total_rows = count * 4 * local_rows
        for part in range(parts):
            answer = jnp.dot(
                inner_ref[0:total_rows, :],
                down_mats[:, part * part_width : (part + 1) * part_width],
                preferred_element_type=jnp.float32,
            ).reshape(count, 2, 2, local_rows, part_width)
            core_out[part, begin : begin + count] = answer[:, :, 1].astype(jnp.bfloat16)
            send(
                core_out.at[part, steps],
                core_in.at[part, steps],
                core_send.at[group, part],
                core_recv.at[group, part],
                mate,
            )
            kept[part, begin : begin + count] = answer[:, :, 0]

    def add_core(group):
        begin, count = groups[group]
        steps = pl.ds(begin, count)
        end = begin + count
        for part in range(parts):
            landed(core_in.at[part, steps], core_recv.at[group, part])
            y_out[part, begin:end] = (
                kept[part, begin:end, 1] + core_in[part, begin:end, 1].astype(jnp.float32)
            ).astype(jnp.bfloat16)
            send(
                y_out.at[part, steps],
                y_in.at[part, steps],
                y_send.at[group, part],
                y_recv.at[group, part],
                y_peer,
            )
            kept[part, begin:end, 0] = (
                kept[part, begin:end, 0] + core_in[part, begin:end, 0].astype(jnp.float32)
            )

    def add_y(group):
        begin, count = groups[group]
        for part in range(parts):
            landed(y_in.at[part, pl.ds(begin, count)], y_recv.at[group, part])
            for step in range(begin, begin + count):
                total = kept[part, step, 0] + y_in[part, step].astype(jnp.float32)
                if step == 0:
                    kept[part, 0, 0] = total
                else:
                    z_out[part, step] = total.astype(jnp.bfloat16)
                    send(
                        z_out.at[part, step],
                        z_in.at[part, step],
                        z_send.at[step, part],
                        z_recv.at[step, part],
                        z_peer(depth - step),
                    )

    for step in range(1, depth):
        rows_to_z(step)
    rows_to_y(0)
    rows_to_mate(0, 0)
    from_y(0)
    from_z(1)
    from_z(2)
    from_y(1)
    for load in loads:
        load.wait()
    for group, (begin, count) in enumerate(groups):
        first(group)
        if group >= 1:
            add_y(group - 1)
        from_z(begin + 3)
        from_y(begin + 2)
        down(group)
        add_core(group)
        from_z(begin + 4)
        from_y(begin + 3)
    add_y(len(groups) - 1)

    for part in range(parts):
        columns = slice(part * part_width, (part + 1) * part_width)
        total = residual_ref[:, columns].astype(jnp.float32) + kept[part, 0, 0]
        for step in range(1, depth):
            landed(z_in.at[part, step], z_recv.at[step, part])
            total = total + z_in[part, step].astype(jnp.float32)
        out_ref[:, columns] = total.astype(out_ref.dtype)
    for copy in started:
        copy.wait_send()


def dense_mixture(residual, norm_gain, expert_ids, route_weights, w_gate, w_up, w_down):
    local_rows, width = residual.shape
    half = w_gate.shape[3]
    choices = expert_ids.shape[1]
    device_total = lax.axis_size("ep")
    depth = device_total // 4
    groups = [(begin, min(2, depth - begin)) for begin in range(0, depth, 2)]
    parts = 4
    part_width = width // parts
    dma = pltpu.SemaphoreType.DMA
    bf16 = jnp.bfloat16
    vmem = pl.BlockSpec(memory_space=pltpu.VMEM)
    anywhere = pl.BlockSpec(memory_space=pl.ANY)
    flops = 2 * device_total * local_rows * width * half * 6
    return pl.pallas_call(
        functools.partial(mixture_kernel, depth, groups, parts),
        out_shape=jax.ShapeDtypeStruct(residual.shape, residual.dtype),
        in_specs=[anywhere] * 7,
        out_specs=vmem,
        scratch_shapes=[
            pltpu.VMEM((local_rows, width), bf16),
            pltpu.VMEM((width // LANES, LANES), bf16),
            pltpu.VMEM((choices, local_rows), jnp.int32),
            pltpu.VMEM((choices, local_rows), jnp.float32),
            pltpu.VMEM((width, 4 * half), bf16),
            pltpu.VMEM((2 * half, width), bf16),
            pltpu.VMEM((depth, 2, 2, local_rows, width + LANES), bf16),
            pltpu.VMEM((8 * local_rows, 2 * half), bf16),
            pltpu.VMEM((parts, depth, 2, local_rows, part_width), jnp.float32),
            pltpu.VMEM((parts, depth, 2, local_rows, part_width), bf16),
            pltpu.VMEM((parts, depth, 2, local_rows, part_width), bf16),
            pltpu.VMEM((parts, depth, local_rows, part_width), bf16),
            pltpu.VMEM((parts, depth, local_rows, part_width), bf16),
            pltpu.VMEM((parts, depth, local_rows, part_width), bf16),
            pltpu.VMEM((parts, depth, local_rows, part_width), bf16),
            dma((4,)),
            dma((6,)),
            dma((depth, 2, 2)),
            dma((depth,)),
            dma((depth,)),
            dma((depth, 2)),
            dma((len(groups), parts)),
            dma((len(groups), parts)),
            dma((len(groups), parts)),
            dma((len(groups), parts)),
            dma((depth, parts)),
            dma((depth, parts)),
        ],
        compiler_params=pltpu.CompilerParams(
            collective_id=0, has_side_effects=True, vmem_limit_bytes=62 * 2**20
        ),
        cost_estimate=pl.CostEstimate(
            flops=flops, bytes_accessed=12 * width * half, transcendentals=0
        ),
    )(
        residual,
        norm_gain.reshape(width // LANES, LANES),
        expert_ids.T,
        route_weights.T,
        w_gate,
        w_up,
        w_down,
    )


def local(residual, norm_gain, expert_ids, route_weights, w_gate, w_up, w_down):
    local_rows = residual.shape[0]
    model_width = residual.shape[1]
    device_total = lax.axis_size("ep")
    block_total = device_total // 2
    typical = max(1, local_rows * TOP // device_total)
    pair_slots = min(local_rows, 4 * typical)
    if pair_slots == local_rows and device_total % 4 == 0 and device_total <= LANES:
        return dense_mixture(
            residual, norm_gain, expert_ids, route_weights, w_gate, w_up, w_down
        )
    widened = residual.astype(jnp.float32)
    scaling = lax.rsqrt(jnp.mean(widened * widened, axis=1, keepdims=True) + 1e-06)
    normed = (widened * scaling * norm_gain.astype(jnp.float32)[None, :]).astype(jnp.bfloat16)
    shares = (route_weights / jnp.sum(route_weights, axis=1, keepdims=True)).astype(jnp.bfloat16)

    def weighted_both(arrived, arrived_weights):
        flat_rows = arrived.reshape(-1, arrived.shape[2])
        flat_weights = arrived_weights.reshape(-1, 2).astype(jnp.float32)
        mixed = flat_weights[:, 0:1] * half_ffn(flat_rows, w_gate[0, 0], w_up[0, 0], w_down[0, 0])
        mixed = mixed + flat_weights[:, 1:2] * half_ffn(
            flat_rows, w_gate[0, 1], w_up[0, 1], w_down[0, 1]
        )
        return mixed.reshape(arrived.shape)

    half_slots = (pair_slots + 1) // 2
    padded_slots = 2 * half_slots
    picker, slot_rows, slot_weights = pair_tables(
        expert_ids, shares, normed, block_total, padded_slots
    )
    outgoing = slot_rows.reshape(device_total, half_slots, model_width)
    weights_out = slot_weights.reshape(device_total, half_slots, 2)
    arrived = lax.all_to_all(outgoing, "ep", split_axis=0, concat_axis=0, tiled=True)
    arrived_weights = lax.all_to_all(weights_out, "ep", split_axis=0, concat_axis=0, tiled=True)
    other_rows, other_weights = swapped((arrived, arrived_weights), "ep", 0)
    mine = weighted_both(arrived, arrived_weights)
    theirs = weighted_both(other_rows, other_weights)
    back = swapped(theirs, "ep", 0)
    answered = mine + back
    returned = lax.all_to_all(answered, "ep", split_axis=0, concat_axis=0, tiled=True)
    pooled = returned.reshape(block_total * padded_slots, model_width)
    combined = jnp.dot(picker.astype(jnp.float32), pooled, precision=lax.Precision.HIGHEST)
    return (widened + combined).astype(jnp.bfloat16)


def solution(mesh):
    placed = (
        P(("groups", "ep"), None),
        P(),
        P(("groups", "ep"), None),
        P(("groups", "ep"), None),
        P("ep", None, None, None),
        P("ep", None, None, None),
        P("ep", None, None, None),
    )
    return jax.shard_map(
        local, mesh=mesh, in_specs=placed, out_specs=P(("groups", "ep"), None), check_vma=False
    )
```

```python
import functools

import jax
import jax.numpy as jnp
from jax import lax
from jax.experimental import pallas as pl
from jax.experimental.pallas import tpu as pltpu
from jax.sharding import PartitionSpec as P

TOP = 8


def swapped(value, axis, distance):
    mask = 2**distance
    pairs = [(source, source ^ mask) for source in range(lax.axis_size(axis))]
    return lax.ppermute(value, axis, pairs)


def half_ffn(inputs, gate_mat, up_mat, down_mat):
    gate_part = jnp.dot(inputs, gate_mat, preferred_element_type=jnp.float32)
    upper = jnp.dot(inputs, up_mat, preferred_element_type=jnp.float32)
    inner = (jax.nn.silu(gate_part) * upper).astype(jnp.bfloat16)
    return jnp.dot(inner, down_mat, preferred_element_type=jnp.float32)


def pair_tables(expert_ids, shares, normed, block_total, slot_total):
    local_rows = normed.shape[0]
    expert_total = 2 * block_total
    block_iota = lax.broadcasted_iota(jnp.int32, (1, 1, block_total), 2)
    block_hits = jnp.any((expert_ids // 2)[:, :, None] == block_iota, axis=1).astype(jnp.int32)
    block_rank = jnp.cumsum(block_hits, axis=0) - 1
    hit_wide = jnp.repeat(block_hits, slot_total, axis=1)
    rank_wide = jnp.repeat(block_rank, slot_total, axis=1)
    slot_place = lax.broadcasted_iota(jnp.int32, (1, block_total * slot_total), 1) % slot_total
    picker = jnp.logical_and(hit_wide > 0, rank_wide == slot_place)
    expert_iota = lax.broadcasted_iota(jnp.int32, (1, 1, expert_total), 2)
    expert_mask = expert_ids[:, :, None] == expert_iota
    share_table = jnp.sum(
        jnp.where(expert_mask, shares[:, :, None], jnp.zeros((), jnp.bfloat16)), axis=1
    )
    share_wide = jnp.repeat(share_table.reshape(local_rows, block_total, 2), slot_total, axis=1)
    slot_weights = jnp.sum(
        jnp.where(picker[:, :, None], share_wide, jnp.zeros((), jnp.bfloat16)), axis=0
    )
    slot_rows = jnp.einsum(
        "rs,rd->sd", picker.astype(jnp.bfloat16), normed, preferred_element_type=jnp.float32
    ).astype(jnp.bfloat16)
    return (picker, slot_rows, slot_weights)


LANES = 128


def mixture_kernel(
    depth,
    groups,
    parts,
    residual_hbm,
    gain_hbm,
    ids_hbm,
    weights_hbm,
    gate_hbm,
    up_hbm,
    down_hbm,
    out_ref,
    residual_ref,
    gain_ref,
    ids_ref,
    weights_ref,
    first_mats,
    down_mats,
    rows,
    inner_ref,
    kept,
    core_out,
    core_in,
    y_out,
    y_in,
    z_out,
    z_in,
    small_sems,
    weight_sems,
    rows_recv,
    rows_z_send,
    rows_y_send,
    rows_core_send,
    core_send,
    core_recv,
    y_send,
    y_recv,
    z_send,
    z_recv,
):
    place = lax.axis_index("ep")
    core = place % 2
    chip = place // 2
    y_at = chip % 2
    z_at = chip // 2
    mate = place + 1 - 2 * core
    y_peer = place + 2 - 4 * y_at

    def z_peer(step):
        return ((z_at + step + 1) % depth) * 4 + y_at * 2 + core

    def z_source(step):
        return ((z_at + depth - step - 1) % depth) * 4 + y_at * 2 + core

    own = depth - 1

    local_rows, width = residual_ref.shape
    part_width = width // parts
    half = gate_hbm.shape[3]
    hidden = 2 * half

    smalls = []
    for which, (source, target) in enumerate(
        (
            (residual_hbm, residual_ref),
            (gain_hbm, gain_ref),
            (ids_hbm, ids_ref),
            (weights_hbm, weights_ref),
        )
    ):
        smalls.append(pltpu.make_async_copy(source, target, small_sems.at[which]))
    for load in smalls:
        load.start()
    barrier = pltpu.get_barrier_semaphore()
    for peer in [mate, y_peer] + [z_peer(step) for step in range(own)]:
        pl.semaphore_signal(
            barrier, inc=1, device_id={"ep": peer}, device_id_type=pl.DeviceIdType.MESH
        )

    loads = []
    for member in range(2):
        for which, source in enumerate((gate_hbm, up_hbm)):
            loads.append(
                pltpu.make_async_copy(
                    source.at[0, member],
                    first_mats.at[:, pl.ds(which * hidden + member * half, half)],
                    weight_sems.at[2 * member + which],
                )
            )
    for member in range(2):
        loads.append(
            pltpu.make_async_copy(
                down_hbm.at[0, member],
                down_mats.at[pl.ds(member * half, half), :],
                weight_sems.at[4 + member],
            )
        )
    for load in loads:
        load.start()
    for load in smalls:
        load.wait()

    widened = residual_ref[...].astype(jnp.float32)
    scaling = lax.rsqrt(jnp.mean(widened * widened, axis=1, keepdims=True) + 1e-06)
    for block in range(width // LANES):
        columns = slice(block * LANES, (block + 1) * LANES)
        gain = gain_ref[block : block + 1, :].astype(jnp.float32)
        rows[own, 0, 0, :, columns] = (widened[:, columns] * scaling * gain).astype(jnp.bfloat16)
    route = weights_ref[...]
    shares = (route / jnp.sum(route, axis=0, keepdims=True)).astype(jnp.bfloat16).astype(jnp.float32)
    ids = ids_ref[...]
    expert = lax.broadcasted_iota(jnp.int32, (LANES, local_rows), 0)
    table = jnp.zeros((LANES, local_rows), jnp.float32)
    for choice in range(ids.shape[0]):
        table = table + jnp.where(
            ids[choice : choice + 1, :] == expert, shares[choice : choice + 1, :], 0.0
        )
    same = lax.broadcasted_iota(jnp.int32, (local_rows, local_rows), 0) == (
        lax.broadcasted_iota(jnp.int32, (local_rows, local_rows), 1)
    )
    turned = lax.dot_general(
        same.astype(jnp.float32).astype(jnp.bfloat16),
        table.astype(jnp.bfloat16),
        (((1,), (1,)), ((), ())),
        preferred_element_type=jnp.float32,
    )
    rows[own, 0, 0, :, width : width + LANES] = turned.astype(jnp.bfloat16)

    pl.semaphore_wait(barrier, depth + 1)

    started = []

    def send(source, target, send_sem, recv_sem, peer):
        copy = pltpu.make_async_remote_copy(
            src_ref=source,
            dst_ref=target,
            send_sem=send_sem,
            recv_sem=recv_sem,
            device_id={"ep": peer},
            device_id_type=pl.DeviceIdType.MESH,
        )
        copy.start()
        started.append(copy)

    def landed(buffer, sem):
        pltpu.make_async_copy(buffer, buffer, sem).wait()

    def arrived(step, dy, dc):
        landed(rows.at[step, dy, dc], rows_recv.at[step, dy, dc])

    def rows_to_z(step):
        send(
            rows.at[own, 0, 0],
            rows.at[step, 0, 0],
            rows_z_send.at[step],
            rows_recv.at[step, 0, 0],
            z_peer(step),
        )

    def rows_to_y(step):
        send(
            rows.at[step, 0, 0],
            rows.at[step, 1, 0],
            rows_y_send.at[step],
            rows_recv.at[step, 1, 0],
            y_peer,
        )

    def rows_to_mate(step, dy):
        send(
            rows.at[step, dy, 0],
            rows.at[step, dy, 1],
            rows_core_send.at[step, dy],
            rows_recv.at[step, dy, 1],
            mate,
        )

    def from_z(step):
        arrived(step, 0, 0)
        rows_to_y(step)
        rows_to_mate(step, 0)

    def from_y(step):
        arrived(step, 1, 0)
        rows_to_mate(step, 1)

    def first(group):
        begin, count = groups[group]
        for step in range(begin, begin + count):
            arrived(step, 0, 1)
            arrived(step, 1, 1)
        total_rows = count * 4 * local_rows
        block = rows[begin : begin + count, :, :, :, 0:width].reshape(total_rows, width)
        shares_here = rows[begin : begin + count, :, :, :, width : width + LANES]
        shares_here = shares_here.reshape(total_rows, LANES).astype(jnp.float32)
        lanes = lax.broadcasted_iota(jnp.int32, (total_rows, LANES), 1)
        both = jnp.dot(block, first_mats[...], preferred_element_type=jnp.float32)
        for member in range(2):
            share = jnp.sum(
                jnp.where(lanes == 2 * chip + member, shares_here, 0.0), axis=1, keepdims=True
            )
            gate_part = both[:, member * half : (member + 1) * half]
            upper = both[:, hidden + member * half : hidden + (member + 1) * half]
            inner = (jax.nn.silu(gate_part) * upper).astype(jnp.bfloat16)
            inner_ref[0:total_rows, member * half : (member + 1) * half] = (
                inner.astype(jnp.float32) * share
            ).astype(jnp.bfloat16)

    def down(group):
        begin, count = groups[group]
        steps = pl.ds(begin, count)
        total_rows = count * 4 * local_rows
        for part in range(parts):
            answer = jnp.dot(
                inner_ref[0:total_rows, :],
                down_mats[:, part * part_width : (part + 1) * part_width],
                preferred_element_type=jnp.float32,
            ).reshape(count, 2, 2, local_rows, part_width)
            core_out[part, begin : begin + count] = answer[:, :, 1].astype(jnp.bfloat16)
            send(
                core_out.at[part, steps],
                core_in.at[part, steps],
                core_send.at[group, part],
                core_recv.at[group, part],
                mate,
            )
            kept[part, begin : begin + count] = answer[:, :, 0]

    def add_core(group):
        begin, count = groups[group]
        steps = pl.ds(begin, count)
        end = begin + count
        for part in range(parts):
            landed(core_in.at[part, steps], core_recv.at[group, part])
            y_out[part, begin:end] = (
                kept[part, begin:end, 1] + core_in[part, begin:end, 1].astype(jnp.float32)
            ).astype(jnp.bfloat16)
            send(
                y_out.at[part, steps],
                y_in.at[part, steps],
                y_send.at[group, part],
                y_recv.at[group, part],
                y_peer,
            )
            kept[part, begin:end, 0] = (
                kept[part, begin:end, 0] + core_in[part, begin:end, 0].astype(jnp.float32)
            )

    def add_y(group):
        begin, count = groups[group]
        for part in range(parts):
            landed(y_in.at[part, pl.ds(begin, count)], y_recv.at[group, part])
            for step in range(begin, begin + count):
                total = kept[part, step, 0] + y_in[part, step].astype(jnp.float32)
                if step == own:
                    kept[part, own, 0] = total
                else:
                    z_out[part, step] = total.astype(jnp.bfloat16)
                    send(
                        z_out.at[part, step],
                        z_in.at[part, step],
                        z_send.at[step, part],
                        z_recv.at[step, part],
                        z_source(step),
                    )

    order = sorted(range(own), key=lambda step: abs(2 * (step + 1) - depth))
    for step in order:
        rows_to_z(step)
    rows_to_y(own)
    rows_to_mate(own, 0)
    from_y(own)
    for index, step in enumerate(order):
        from_z(step)
        if index >= 1:
            from_y(order[index - 1])
    for load in loads:
        load.wait()
    for group in range(len(groups)):
        if group == len(groups) - 1 and len(groups) == 1:
            from_y(order[-1])
        first(group)
        if group == 0 and len(groups) > 1:
            from_y(order[-1])
        if group >= 1:
            add_y(group - 1)
        down(group)
        add_core(group)
    add_y(len(groups) - 1)

    for part in range(parts):
        columns = slice(part * part_width, (part + 1) * part_width)
        total = residual_ref[:, columns].astype(jnp.float32) + kept[part, own, 0]
        for step in range(own):
            landed(z_in.at[part, step], z_recv.at[step, part])
            total = total + z_in[part, step].astype(jnp.float32)
        out_ref[:, columns] = total.astype(out_ref.dtype)
    for copy in started:
        copy.wait_send()


def dense_mixture(residual, norm_gain, expert_ids, route_weights, w_gate, w_up, w_down):
    local_rows, width = residual.shape
    half = w_gate.shape[3]
    choices = expert_ids.shape[1]
    device_total = lax.axis_size("ep")
    depth = device_total // 4
    groups = [(begin, min(2, depth - begin)) for begin in range(0, depth, 2)]
    parts = 4
    part_width = width // parts
    dma = pltpu.SemaphoreType.DMA
    bf16 = jnp.bfloat16
    vmem = pl.BlockSpec(memory_space=pltpu.VMEM)
    anywhere = pl.BlockSpec(memory_space=pl.ANY)
    flops = 2 * device_total * local_rows * width * half * 6
    return pl.pallas_call(
        functools.partial(mixture_kernel, depth, groups, parts),
        out_shape=jax.ShapeDtypeStruct(residual.shape, residual.dtype),
        in_specs=[anywhere] * 7,
        out_specs=vmem,
        scratch_shapes=[
            pltpu.VMEM((local_rows, width), bf16),
            pltpu.VMEM((width // LANES, LANES), bf16),
            pltpu.VMEM((choices, local_rows), jnp.int32),
            pltpu.VMEM((choices, local_rows), jnp.float32),
            pltpu.VMEM((width, 4 * half), bf16),
            pltpu.VMEM((2 * half, width), bf16),
            pltpu.VMEM((depth, 2, 2, local_rows, width + LANES), bf16),
            pltpu.VMEM((8 * local_rows, 2 * half), bf16),
            pltpu.VMEM((parts, depth, 2, local_rows, part_width), jnp.float32),
            pltpu.VMEM((parts, depth, 2, local_rows, part_width), bf16),
            pltpu.VMEM((parts, depth, 2, local_rows, part_width), bf16),
            pltpu.VMEM((parts, depth, local_rows, part_width), bf16),
            pltpu.VMEM((parts, depth, local_rows, part_width), bf16),
            pltpu.VMEM((parts, depth, local_rows, part_width), bf16),
            pltpu.VMEM((parts, depth, local_rows, part_width), bf16),
            dma((4,)),
            dma((6,)),
            dma((depth, 2, 2)),
            dma((depth,)),
            dma((depth,)),
            dma((depth, 2)),
            dma((len(groups), parts)),
            dma((len(groups), parts)),
            dma((len(groups), parts)),
            dma((len(groups), parts)),
            dma((depth, parts)),
            dma((depth, parts)),
        ],
        compiler_params=pltpu.CompilerParams(
            collective_id=0, has_side_effects=True, vmem_limit_bytes=62 * 2**20
        ),
        cost_estimate=pl.CostEstimate(
            flops=flops, bytes_accessed=12 * width * half, transcendentals=0
        ),
    )(
        residual,
        norm_gain.reshape(width // LANES, LANES),
        expert_ids.T,
        route_weights.T,
        w_gate,
        w_up,
        w_down,
    )


def local(residual, norm_gain, expert_ids, route_weights, w_gate, w_up, w_down):
    local_rows = residual.shape[0]
    model_width = residual.shape[1]
    device_total = lax.axis_size("ep")
    block_total = device_total // 2
    typical = max(1, local_rows * TOP // device_total)
    pair_slots = min(local_rows, 4 * typical)
    if pair_slots == local_rows and device_total % 8 == 0 and device_total <= LANES:
        return dense_mixture(
            residual, norm_gain, expert_ids, route_weights, w_gate, w_up, w_down
        )
    widened = residual.astype(jnp.float32)
    scaling = lax.rsqrt(jnp.mean(widened * widened, axis=1, keepdims=True) + 1e-06)
    normed = (widened * scaling * norm_gain.astype(jnp.float32)[None, :]).astype(jnp.bfloat16)
    shares = (route_weights / jnp.sum(route_weights, axis=1, keepdims=True)).astype(jnp.bfloat16)

    def weighted_both(arrived, arrived_weights):
        flat_rows = arrived.reshape(-1, arrived.shape[2])
        flat_weights = arrived_weights.reshape(-1, 2).astype(jnp.float32)
        mixed = flat_weights[:, 0:1] * half_ffn(flat_rows, w_gate[0, 0], w_up[0, 0], w_down[0, 0])
        mixed = mixed + flat_weights[:, 1:2] * half_ffn(
            flat_rows, w_gate[0, 1], w_up[0, 1], w_down[0, 1]
        )
        return mixed.reshape(arrived.shape)

    half_slots = (pair_slots + 1) // 2
    padded_slots = 2 * half_slots
    picker, slot_rows, slot_weights = pair_tables(
        expert_ids, shares, normed, block_total, padded_slots
    )
    outgoing = slot_rows.reshape(device_total, half_slots, model_width)
    weights_out = slot_weights.reshape(device_total, half_slots, 2)
    arrived = lax.all_to_all(outgoing, "ep", split_axis=0, concat_axis=0, tiled=True)
    arrived_weights = lax.all_to_all(weights_out, "ep", split_axis=0, concat_axis=0, tiled=True)
    other_rows, other_weights = swapped((arrived, arrived_weights), "ep", 0)
    mine = weighted_both(arrived, arrived_weights)
    theirs = weighted_both(other_rows, other_weights)
    back = swapped(theirs, "ep", 0)
    answered = mine + back
    returned = lax.all_to_all(answered, "ep", split_axis=0, concat_axis=0, tiled=True)
    pooled = returned.reshape(block_total * padded_slots, model_width)
    combined = jnp.dot(picker.astype(jnp.float32), pooled, precision=lax.Precision.HIGHEST)
    return (widened + combined).astype(jnp.bfloat16)


def solution(mesh):
    placed = (
        P(("groups", "ep"), None),
        P(),
        P(("groups", "ep"), None),
        P(("groups", "ep"), None),
        P("ep", None, None, None),
        P("ep", None, None, None),
        P("ep", None, None, None),
    )
    return jax.shard_map(
        local, mesh=mesh, in_specs=placed, out_specs=P(("groups", "ep"), None), check_vma=False
    )
```

```python
import functools

import jax
import jax.numpy as jnp
from jax import lax
from jax.experimental import pallas as pl
from jax.experimental.pallas import tpu as pltpu
from jax.sharding import PartitionSpec as P

TOP = 8


def swapped(value, axis, distance):
    mask = 2**distance
    pairs = [(source, source ^ mask) for source in range(lax.axis_size(axis))]
    return lax.ppermute(value, axis, pairs)


def half_ffn(inputs, gate_mat, up_mat, down_mat):
    gate_part = jnp.dot(inputs, gate_mat, preferred_element_type=jnp.float32)
    upper = jnp.dot(inputs, up_mat, preferred_element_type=jnp.float32)
    inner = (jax.nn.silu(gate_part) * upper).astype(jnp.bfloat16)
    return jnp.dot(inner, down_mat, preferred_element_type=jnp.float32)


def pair_tables(expert_ids, shares, normed, block_total, slot_total):
    local_rows = normed.shape[0]
    expert_total = 2 * block_total
    block_iota = lax.broadcasted_iota(jnp.int32, (1, 1, block_total), 2)
    block_hits = jnp.any((expert_ids // 2)[:, :, None] == block_iota, axis=1).astype(jnp.int32)
    block_rank = jnp.cumsum(block_hits, axis=0) - 1
    hit_wide = jnp.repeat(block_hits, slot_total, axis=1)
    rank_wide = jnp.repeat(block_rank, slot_total, axis=1)
    slot_place = lax.broadcasted_iota(jnp.int32, (1, block_total * slot_total), 1) % slot_total
    picker = jnp.logical_and(hit_wide > 0, rank_wide == slot_place)
    expert_iota = lax.broadcasted_iota(jnp.int32, (1, 1, expert_total), 2)
    expert_mask = expert_ids[:, :, None] == expert_iota
    share_table = jnp.sum(
        jnp.where(expert_mask, shares[:, :, None], jnp.zeros((), jnp.bfloat16)), axis=1
    )
    share_wide = jnp.repeat(share_table.reshape(local_rows, block_total, 2), slot_total, axis=1)
    slot_weights = jnp.sum(
        jnp.where(picker[:, :, None], share_wide, jnp.zeros((), jnp.bfloat16)), axis=0
    )
    slot_rows = jnp.einsum(
        "rs,rd->sd", picker.astype(jnp.bfloat16), normed, preferred_element_type=jnp.float32
    ).astype(jnp.bfloat16)
    return (picker, slot_rows, slot_weights)


LANES = 128


def mixture_kernel(
    depth,
    groups,
    parts,
    residual_hbm,
    gain_hbm,
    ids_hbm,
    weights_hbm,
    gate_hbm,
    up_hbm,
    down_hbm,
    out_ref,
    residual_ref,
    gain_ref,
    ids_ref,
    weights_ref,
    first_mats,
    down_mats,
    rows,
    inner_ref,
    kept,
    core_out,
    core_in,
    y_out,
    y_in,
    z_out,
    z_in,
    small_sems,
    weight_sems,
    rows_recv,
    rows_z_send,
    rows_y_send,
    rows_core_send,
    core_send,
    core_recv,
    y_send,
    y_recv,
    z_send,
    z_recv,
):
    place = lax.axis_index("ep")
    core = place % 2
    chip = place // 2
    y_at = chip % 2
    z_at = chip // 2
    mate = place + 1 - 2 * core
    y_peer = place + 2 - 4 * y_at

    def z_peer(step):
        return ((z_at + step) % depth) * 4 + y_at * 2 + core

    local_rows, width = residual_ref.shape
    part_width = width // parts
    half = gate_hbm.shape[3]
    hidden = 2 * half

    smalls = []
    for which, (source, target) in enumerate(
        (
            (residual_hbm, residual_ref),
            (gain_hbm, gain_ref),
            (ids_hbm, ids_ref),
            (weights_hbm, weights_ref),
        )
    ):
        smalls.append(pltpu.make_async_copy(source, target, small_sems.at[which]))
    for load in smalls:
        load.start()

    barrier = pltpu.get_barrier_semaphore()
    for peer in [mate, y_peer] + [z_peer(step) for step in range(1, depth)]:
        pl.semaphore_signal(
            barrier, inc=1, device_id={"ep": peer}, device_id_type=pl.DeviceIdType.MESH
        )

    loads = []
    for member in range(2):
        for which, source in enumerate((gate_hbm, up_hbm)):
            loads.append(
                pltpu.make_async_copy(
                    source.at[0, member],
                    first_mats.at[:, pl.ds(which * hidden + member * half, half)],
                    weight_sems.at[2 * member + which],
                )
            )
    for member in range(2):
        loads.append(
            pltpu.make_async_copy(
                down_hbm.at[0, member],
                down_mats.at[pl.ds(member * half, half), :],
                weight_sems.at[4 + member],
            )
        )
    for load in smalls:
        load.wait()

    widened = residual_ref[...].astype(jnp.float32)
    scaling = lax.rsqrt(jnp.mean(widened * widened, axis=1, keepdims=True) + 1e-06)
    for block in range(width // LANES):
        columns = slice(block * LANES, (block + 1) * LANES)
        gain = gain_ref[block : block + 1, :].astype(jnp.float32)
        rows[0, 0, 0, :, columns] = (widened[:, columns] * scaling * gain).astype(jnp.bfloat16)
    route = weights_ref[...]
    shares = (route / jnp.sum(route, axis=0, keepdims=True)).astype(jnp.bfloat16).astype(jnp.float32)
    ids = ids_ref[...]
    expert = lax.broadcasted_iota(jnp.int32, (LANES, local_rows), 0)
    table = jnp.zeros((LANES, local_rows), jnp.float32)
    for choice in range(ids.shape[0]):
        table = table + jnp.where(
            ids[choice : choice + 1, :] == expert, shares[choice : choice + 1, :], 0.0
        )
    same = lax.broadcasted_iota(jnp.int32, (local_rows, local_rows), 0) == (
        lax.broadcasted_iota(jnp.int32, (local_rows, local_rows), 1)
    )
    turned = lax.dot_general(
        same.astype(jnp.float32).astype(jnp.bfloat16),
        table.astype(jnp.bfloat16),
        (((1,), (1,)), ((), ())),
        preferred_element_type=jnp.float32,
    )
    rows[0, 0, 0, :, width : width + LANES] = turned.astype(jnp.bfloat16)

    pl.semaphore_wait(barrier, depth + 1)

    started = []

    def send(source, target, send_sem, recv_sem, peer):
        copy = pltpu.make_async_remote_copy(
            src_ref=source,
            dst_ref=target,
            send_sem=send_sem,
            recv_sem=recv_sem,
            device_id={"ep": peer},
            device_id_type=pl.DeviceIdType.MESH,
        )
        copy.start()
        started.append(copy)

    def landed(buffer, sem):
        pltpu.make_async_copy(buffer, buffer, sem).wait()

    def arrived(step, dy, dc):
        landed(rows.at[step, dy, dc], rows_recv.at[step, dy, dc])

    def rows_to_z(step):
        send(
            rows.at[0, 0, 0],
            rows.at[step, 0, 0],
            rows_z_send.at[step],
            rows_recv.at[step, 0, 0],
            z_peer(step),
        )

    def rows_to_y(step):
        send(
            rows.at[step, 0, 0],
            rows.at[step, 1, 0],
            rows_y_send.at[step],
            rows_recv.at[step, 1, 0],
            y_peer,
        )

    def rows_to_mate(step, dy):
        send(
            rows.at[step, dy, 0],
            rows.at[step, dy, 1],
            rows_core_send.at[step, dy],
            rows_recv.at[step, dy, 1],
            mate,
        )

    def from_z(step):
        if 0 < step < depth:
            arrived(step, 0, 0)
            rows_to_y(step)
            rows_to_mate(step, 0)

    def from_y(step):
        if step < depth:
            arrived(step, 1, 0)
            rows_to_mate(step, 1)

    def first(group):
        begin, count = groups[group]
        for step in range(begin, begin + count):
            arrived(step, 0, 1)
            arrived(step, 1, 1)
        total_rows = count * 4 * local_rows
        block = rows[begin : begin + count, :, :, :, 0:width].reshape(total_rows, width)
        shares_here = rows[begin : begin + count, :, :, :, width : width + LANES]
        shares_here = shares_here.reshape(total_rows, LANES).astype(jnp.float32)
        lanes = lax.broadcasted_iota(jnp.int32, (total_rows, LANES), 1)
        both = jnp.dot(block, first_mats[...], preferred_element_type=jnp.float32)
        for member in range(2):
            share = jnp.sum(
                jnp.where(lanes == 2 * chip + member, shares_here, 0.0), axis=1, keepdims=True
            )
            gate_part = both[:, member * half : (member + 1) * half]
            upper = both[:, hidden + member * half : hidden + (member + 1) * half]
            inner = (jax.nn.silu(gate_part) * upper).astype(jnp.bfloat16)
            inner_ref[0:total_rows, member * half : (member + 1) * half] = (
                inner.astype(jnp.float32) * share
            ).astype(jnp.bfloat16)

    def down(group):
        begin, count = groups[group]
        steps = pl.ds(begin, count)
        total_rows = count * 4 * local_rows
        for part in range(parts):
            answer = jnp.dot(
                inner_ref[0:total_rows, :],
                down_mats[:, part * part_width : (part + 1) * part_width],
                preferred_element_type=jnp.float32,
            ).reshape(count, 2, 2, local_rows, part_width)
            core_out[part, begin : begin + count] = answer[:, :, 1].astype(jnp.bfloat16)
            send(
                core_out.at[part, steps],
                core_in.at[part, steps],
                core_send.at[group, part],
                core_recv.at[group, part],
                mate,
            )
            kept[part, begin : begin + count] = answer[:, :, 0]

    def add_core(group):
        begin, count = groups[group]
        steps = pl.ds(begin, count)
        end = begin + count
        for part in range(parts):
            landed(core_in.at[part, steps], core_recv.at[group, part])
            y_out[part, begin:end] = (
                kept[part, begin:end, 1] + core_in[part, begin:end, 1].astype(jnp.float32)
            ).astype(jnp.bfloat16)
            send(
                y_out.at[part, steps],
                y_in.at[part, steps],
                y_send.at[group, part],
                y_recv.at[group, part],
                y_peer,
            )
            kept[part, begin:end, 0] = (
                kept[part, begin:end, 0] + core_in[part, begin:end, 0].astype(jnp.float32)
            )

    def add_y(group):
        begin, count = groups[group]
        for part in range(parts):
            landed(y_in.at[part, pl.ds(begin, count)], y_recv.at[group, part])
            for step in range(begin, begin + count):
                total = kept[part, step, 0] + y_in[part, step].astype(jnp.float32)
                if step == 0:
                    kept[part, 0, 0] = total
                else:
                    z_out[part, step] = total.astype(jnp.bfloat16)
                    send(
                        z_out.at[part, step],
                        z_in.at[part, step],
                        z_send.at[step, part],
                        z_recv.at[step, part],
                        z_peer(depth - step),
                    )

    for step in range(1, depth):
        rows_to_z(step)
    rows_to_y(0)
    rows_to_mate(0, 0)
    for load in loads:
        load.start()
    from_y(0)
    from_z(1)
    from_z(2)
    from_y(1)
    for load in loads:
        load.wait()
    for group, (begin, count) in enumerate(groups):
        first(group)
        if group >= 1:
            add_y(group - 1)
        from_z(begin + 3)
        from_y(begin + 2)
        down(group)
        add_core(group)
        from_z(begin + 4)
        from_y(begin + 3)
    add_y(len(groups) - 1)

    for part in range(parts):
        columns = slice(part * part_width, (part + 1) * part_width)
        total = residual_ref[:, columns].astype(jnp.float32) + kept[part, 0, 0]
        for step in range(1, depth):
            landed(z_in.at[part, step], z_recv.at[step, part])
            total = total + z_in[part, step].astype(jnp.float32)
        out_ref[:, columns] = total.astype(out_ref.dtype)
    for copy in started:
        copy.wait_send()


def dense_mixture(residual, norm_gain, expert_ids, route_weights, w_gate, w_up, w_down):
    local_rows, width = residual.shape
    half = w_gate.shape[3]
    choices = expert_ids.shape[1]
    device_total = lax.axis_size("ep")
    depth = device_total // 4
    groups = [(begin, min(2, depth - begin)) for begin in range(0, depth, 2)]
    parts = 4
    part_width = width // parts
    dma = pltpu.SemaphoreType.DMA
    bf16 = jnp.bfloat16
    vmem = pl.BlockSpec(memory_space=pltpu.VMEM)
    anywhere = pl.BlockSpec(memory_space=pl.ANY)
    flops = 2 * device_total * local_rows * width * half * 6
    return pl.pallas_call(
        functools.partial(mixture_kernel, depth, groups, parts),
        out_shape=jax.ShapeDtypeStruct(residual.shape, residual.dtype),
        in_specs=[anywhere] * 7,
        out_specs=vmem,
        scratch_shapes=[
            pltpu.VMEM((local_rows, width), bf16),
            pltpu.VMEM((width // LANES, LANES), bf16),
            pltpu.VMEM((choices, local_rows), jnp.int32),
            pltpu.VMEM((choices, local_rows), jnp.float32),
            pltpu.VMEM((width, 4 * half), bf16),
            pltpu.VMEM((2 * half, width), bf16),
            pltpu.VMEM((depth, 2, 2, local_rows, width + LANES), bf16),
            pltpu.VMEM((8 * local_rows, 2 * half), bf16),
            pltpu.VMEM((parts, depth, 2, local_rows, part_width), jnp.float32),
            pltpu.VMEM((parts, depth, 2, local_rows, part_width), bf16),
            pltpu.VMEM((parts, depth, 2, local_rows, part_width), bf16),
            pltpu.VMEM((parts, depth, local_rows, part_width), bf16),
            pltpu.VMEM((parts, depth, local_rows, part_width), bf16),
            pltpu.VMEM((parts, depth, local_rows, part_width), bf16),
            pltpu.VMEM((parts, depth, local_rows, part_width), bf16),
            dma((4,)),
            dma((6,)),
            dma((depth, 2, 2)),
            dma((depth,)),
            dma((depth,)),
            dma((depth, 2)),
            dma((len(groups), parts)),
            dma((len(groups), parts)),
            dma((len(groups), parts)),
            dma((len(groups), parts)),
            dma((depth, parts)),
            dma((depth, parts)),
        ],
        compiler_params=pltpu.CompilerParams(
            collective_id=0, has_side_effects=True, vmem_limit_bytes=62 * 2**20
        ),
        cost_estimate=pl.CostEstimate(
            flops=flops, bytes_accessed=12 * width * half, transcendentals=0
        ),
    )(
        residual,
        norm_gain.reshape(width // LANES, LANES),
        expert_ids.T,
        route_weights.T,
        w_gate,
        w_up,
        w_down,
    )


def local(residual, norm_gain, expert_ids, route_weights, w_gate, w_up, w_down):
    local_rows = residual.shape[0]
    model_width = residual.shape[1]
    device_total = lax.axis_size("ep")
    block_total = device_total // 2
    typical = max(1, local_rows * TOP // device_total)
    pair_slots = min(local_rows, 4 * typical)
    if pair_slots == local_rows and device_total % 4 == 0 and device_total <= LANES:
        return dense_mixture(
            residual, norm_gain, expert_ids, route_weights, w_gate, w_up, w_down
        )
    widened = residual.astype(jnp.float32)
    scaling = lax.rsqrt(jnp.mean(widened * widened, axis=1, keepdims=True) + 1e-06)
    normed = (widened * scaling * norm_gain.astype(jnp.float32)[None, :]).astype(jnp.bfloat16)
    shares = (route_weights / jnp.sum(route_weights, axis=1, keepdims=True)).astype(jnp.bfloat16)

    def weighted_both(arrived, arrived_weights):
        flat_rows = arrived.reshape(-1, arrived.shape[2])
        flat_weights = arrived_weights.reshape(-1, 2).astype(jnp.float32)
        mixed = flat_weights[:, 0:1] * half_ffn(flat_rows, w_gate[0, 0], w_up[0, 0], w_down[0, 0])
        mixed = mixed + flat_weights[:, 1:2] * half_ffn(
            flat_rows, w_gate[0, 1], w_up[0, 1], w_down[0, 1]
        )
        return mixed.reshape(arrived.shape)

    half_slots = (pair_slots + 1) // 2
    padded_slots = 2 * half_slots
    picker, slot_rows, slot_weights = pair_tables(
        expert_ids, shares, normed, block_total, padded_slots
    )
    outgoing = slot_rows.reshape(device_total, half_slots, model_width)
    weights_out = slot_weights.reshape(device_total, half_slots, 2)
    arrived = lax.all_to_all(outgoing, "ep", split_axis=0, concat_axis=0, tiled=True)
    arrived_weights = lax.all_to_all(weights_out, "ep", split_axis=0, concat_axis=0, tiled=True)
    other_rows, other_weights = swapped((arrived, arrived_weights), "ep", 0)
    mine = weighted_both(arrived, arrived_weights)
    theirs = weighted_both(other_rows, other_weights)
    back = swapped(theirs, "ep", 0)
    answered = mine + back
    returned = lax.all_to_all(answered, "ep", split_axis=0, concat_axis=0, tiled=True)
    pooled = returned.reshape(block_total * padded_slots, model_width)
    combined = jnp.dot(picker.astype(jnp.float32), pooled, precision=lax.Precision.HIGHEST)
    return (widened + combined).astype(jnp.bfloat16)


def solution(mesh):
    placed = (
        P(("groups", "ep"), None),
        P(),
        P(("groups", "ep"), None),
        P(("groups", "ep"), None),
        P("ep", None, None, None),
        P("ep", None, None, None),
        P("ep", None, None, None),
    )
    return jax.shard_map(
        local, mesh=mesh, in_specs=placed, out_specs=P(("groups", "ep"), None), check_vma=False
    )
```

```python
import functools

import jax
import jax.numpy as jnp
from jax import lax
from jax.experimental import pallas as pl
from jax.experimental.pallas import tpu as pltpu
from jax.sharding import PartitionSpec as P

TOP = 8


def swapped(value, axis, distance):
    mask = 2**distance
    pairs = [(source, source ^ mask) for source in range(lax.axis_size(axis))]
    return lax.ppermute(value, axis, pairs)


def half_ffn(inputs, gate_mat, up_mat, down_mat):
    gate_part = jnp.dot(inputs, gate_mat, preferred_element_type=jnp.float32)
    upper = jnp.dot(inputs, up_mat, preferred_element_type=jnp.float32)
    inner = (jax.nn.silu(gate_part) * upper).astype(jnp.bfloat16)
    return jnp.dot(inner, down_mat, preferred_element_type=jnp.float32)


def pair_tables(expert_ids, shares, normed, block_total, slot_total):
    local_rows = normed.shape[0]
    expert_total = 2 * block_total
    block_iota = lax.broadcasted_iota(jnp.int32, (1, 1, block_total), 2)
    block_hits = jnp.any((expert_ids // 2)[:, :, None] == block_iota, axis=1).astype(jnp.int32)
    block_rank = jnp.cumsum(block_hits, axis=0) - 1
    hit_wide = jnp.repeat(block_hits, slot_total, axis=1)
    rank_wide = jnp.repeat(block_rank, slot_total, axis=1)
    slot_place = lax.broadcasted_iota(jnp.int32, (1, block_total * slot_total), 1) % slot_total
    picker = jnp.logical_and(hit_wide > 0, rank_wide == slot_place)
    expert_iota = lax.broadcasted_iota(jnp.int32, (1, 1, expert_total), 2)
    expert_mask = expert_ids[:, :, None] == expert_iota
    share_table = jnp.sum(
        jnp.where(expert_mask, shares[:, :, None], jnp.zeros((), jnp.bfloat16)), axis=1
    )
    share_wide = jnp.repeat(share_table.reshape(local_rows, block_total, 2), slot_total, axis=1)
    slot_weights = jnp.sum(
        jnp.where(picker[:, :, None], share_wide, jnp.zeros((), jnp.bfloat16)), axis=0
    )
    slot_rows = jnp.einsum(
        "rs,rd->sd", picker.astype(jnp.bfloat16), normed, preferred_element_type=jnp.float32
    ).astype(jnp.bfloat16)
    return (picker, slot_rows, slot_weights)


LANES = 128


def mixture_kernel(
    depth,
    groups,
    parts,
    residual_hbm,
    gain_hbm,
    ids_hbm,
    weights_hbm,
    gate_hbm,
    up_hbm,
    down_hbm,
    out_ref,
    residual_ref,
    gain_ref,
    ids_ref,
    weights_ref,
    first_mats,
    down_mats,
    rows,
    inner_ref,
    kept,
    core_out,
    core_in,
    y_out,
    y_in,
    z_out,
    z_in,
    small_sems,
    weight_sems,
    rows_recv,
    rows_z_send,
    rows_y_send,
    rows_core_send,
    core_send,
    core_recv,
    y_send,
    y_recv,
    z_send,
    z_recv,
):
    place = lax.axis_index("ep")
    core = place % 2
    chip = place // 2
    y_at = chip % 2
    z_at = chip // 2
    mate = place + 1 - 2 * core
    y_peer = place + 2 - 4 * y_at

    def z_peer(step):
        return ((z_at + step) % depth) * 4 + y_at * 2 + core

    local_rows, width = residual_ref.shape
    part_width = width // parts
    half = gate_hbm.shape[3]
    hidden = 2 * half

    smalls = []
    for which, (source, target) in enumerate(
        (
            (residual_hbm, residual_ref),
            (gain_hbm, gain_ref),
            (ids_hbm, ids_ref),
            (weights_hbm, weights_ref),
        )
    ):
        smalls.append(pltpu.make_async_copy(source, target, small_sems.at[which]))
    for load in smalls:
        load.start()

    barrier = pltpu.get_barrier_semaphore()
    for peer in [mate, y_peer] + [z_peer(step) for step in range(1, depth)]:
        pl.semaphore_signal(
            barrier, inc=1, device_id={"ep": peer}, device_id_type=pl.DeviceIdType.MESH
        )

    loads = []
    for member in range(2):
        for which, source in enumerate((gate_hbm, up_hbm)):
            loads.append(
                pltpu.make_async_copy(
                    source.at[0, member],
                    first_mats.at[:, pl.ds(which * hidden + member * half, half)],
                    weight_sems.at[2 * member + which],
                )
            )
    for member in range(2):
        loads.append(
            pltpu.make_async_copy(
                down_hbm.at[0, member],
                down_mats.at[pl.ds(member * half, half), :],
                weight_sems.at[4 + member],
            )
        )
    for load in smalls:
        load.wait()

    widened = residual_ref[...].astype(jnp.float32)
    scaling = lax.rsqrt(jnp.mean(widened * widened, axis=1, keepdims=True) + 1e-06)
    for block in range(width // LANES):
        columns = slice(block * LANES, (block + 1) * LANES)
        gain = gain_ref[block : block + 1, :].astype(jnp.float32)
        rows[0, 0, 0, :, columns] = (widened[:, columns] * scaling * gain).astype(jnp.bfloat16)
    route = weights_ref[...]
    shares = (route / jnp.sum(route, axis=0, keepdims=True)).astype(jnp.bfloat16).astype(jnp.float32)
    ids = ids_ref[...]
    expert = lax.broadcasted_iota(jnp.int32, (LANES, local_rows), 0)
    table = jnp.zeros((LANES, local_rows), jnp.float32)
    for choice in range(ids.shape[0]):
        table = table + jnp.where(
            ids[choice : choice + 1, :] == expert, shares[choice : choice + 1, :], 0.0
        )
    same = lax.broadcasted_iota(jnp.int32, (local_rows, local_rows), 0) == (
        lax.broadcasted_iota(jnp.int32, (local_rows, local_rows), 1)
    )
    turned = lax.dot_general(
        same.astype(jnp.float32).astype(jnp.bfloat16),
        table.astype(jnp.bfloat16),
        (((1,), (1,)), ((), ())),
        preferred_element_type=jnp.float32,
    )
    rows[0, 0, 0, :, width : width + LANES] = turned.astype(jnp.bfloat16)

    pl.semaphore_wait(barrier, depth + 1)

    started = []

    def send(source, target, send_sem, recv_sem, peer):
        copy = pltpu.make_async_remote_copy(
            src_ref=source,
            dst_ref=target,
            send_sem=send_sem,
            recv_sem=recv_sem,
            device_id={"ep": peer},
            device_id_type=pl.DeviceIdType.MESH,
        )
        copy.start()
        started.append(copy)

    def landed(buffer, sem):
        pltpu.make_async_copy(buffer, buffer, sem).wait()

    def arrived(step, dy, dc):
        landed(rows.at[step, dy, dc], rows_recv.at[step, dy, dc])

    def rows_to_z(step):
        send(
            rows.at[0, 0, 0],
            rows.at[step, 0, 0],
            rows_z_send.at[step],
            rows_recv.at[step, 0, 0],
            z_peer(step),
        )

    def rows_to_y(step):
        send(
            rows.at[step, 0, 0],
            rows.at[step, 1, 0],
            rows_y_send.at[step],
            rows_recv.at[step, 1, 0],
            y_peer,
        )

    def rows_to_mate(step, dy):
        send(
            rows.at[step, dy, 0],
            rows.at[step, dy, 1],
            rows_core_send.at[step, dy],
            rows_recv.at[step, dy, 1],
            mate,
        )

    def from_z(step):
        if 0 < step < depth:
            arrived(step, 0, 0)
            rows_to_y(step)
            rows_to_mate(step, 0)

    def from_y(step):
        if step < depth:
            arrived(step, 1, 0)
            rows_to_mate(step, 1)

    def first(group):
        begin, count = groups[group]
        for step in range(begin, begin + count):
            arrived(step, 0, 1)
            arrived(step, 1, 1)
        total_rows = count * 4 * local_rows
        block = rows[begin : begin + count, :, :, :, 0:width].reshape(total_rows, width)
        shares_here = rows[begin : begin + count, :, :, :, width : width + LANES]
        shares_here = shares_here.reshape(total_rows, LANES).astype(jnp.float32)
        lanes = lax.broadcasted_iota(jnp.int32, (total_rows, LANES), 1)
        both = jnp.dot(block, first_mats[...], preferred_element_type=jnp.float32)
        for member in range(2):
            share = jnp.sum(
                jnp.where(lanes == 2 * chip + member, shares_here, 0.0), axis=1, keepdims=True
            )
            gate_part = both[:, member * half : (member + 1) * half]
            upper = both[:, hidden + member * half : hidden + (member + 1) * half]
            inner = (jax.nn.silu(gate_part) * upper).astype(jnp.bfloat16)
            inner_ref[0:total_rows, member * half : (member + 1) * half] = (
                inner.astype(jnp.float32) * share
            ).astype(jnp.bfloat16)

    def down(group):
        begin, count = groups[group]
        steps = pl.ds(begin, count)
        total_rows = count * 4 * local_rows
        for part in range(parts):
            answer = jnp.dot(
                inner_ref[0:total_rows, :],
                down_mats[:, part * part_width : (part + 1) * part_width],
                preferred_element_type=jnp.float32,
            ).reshape(count, 2, 2, local_rows, part_width)
            core_out[part, begin : begin + count] = answer[:, :, 1].astype(jnp.bfloat16)
            send(
                core_out.at[part, steps],
                core_in.at[part, steps],
                core_send.at[group, part],
                core_recv.at[group, part],
                mate,
            )
            kept[part, begin : begin + count] = answer[:, :, 0]

    def add_core(group):
        begin, count = groups[group]
        steps = pl.ds(begin, count)
        end = begin + count
        for part in range(parts):
            landed(core_in.at[part, steps], core_recv.at[group, part])
            y_out[part, begin:end] = (
                kept[part, begin:end, 1] + core_in[part, begin:end, 1].astype(jnp.float32)
            ).astype(jnp.bfloat16)
            send(
                y_out.at[part, steps],
                y_in.at[part, steps],
                y_send.at[group, part],
                y_recv.at[group, part],
                y_peer,
            )
            kept[part, begin:end, 0] = (
                kept[part, begin:end, 0] + core_in[part, begin:end, 0].astype(jnp.float32)
            )

    def add_y(group):
        begin, count = groups[group]
        for part in range(parts):
            landed(y_in.at[part, pl.ds(begin, count)], y_recv.at[group, part])
            for step in range(begin, begin + count):
                total = kept[part, step, 0] + y_in[part, step].astype(jnp.float32)
                if step == 0:
                    kept[part, 0, 0] = total
                else:
                    z_out[part, step] = total.astype(jnp.bfloat16)
                    send(
                        z_out.at[part, step],
                        z_in.at[part, step],
                        z_send.at[step, part],
                        z_recv.at[step, part],
                        z_peer(depth - step),
                    )

    for step in range(1, depth):
        rows_to_z(step)
    rows_to_y(0)
    rows_to_mate(0, 0)
    for load in loads:
        load.start()
    from_y(0)
    from_z(1)
    from_z(2)
    from_y(1)
    for load in loads:
        load.wait()
    for group, (begin, count) in enumerate(groups):
        first(group)
        if group >= 1:
            add_y(group - 1)
        from_z(begin + 3)
        from_y(begin + 2)
        down(group)
        add_core(group)
        from_z(begin + 4)
        from_y(begin + 3)
    add_y(len(groups) - 1)

    for part in range(parts):
        columns = slice(part * part_width, (part + 1) * part_width)
        total = residual_ref[:, columns].astype(jnp.float32) + kept[part, 0, 0]
        for step in range(1, depth):
            landed(z_in.at[part, step], z_recv.at[step, part])
            total = total + z_in[part, step].astype(jnp.float32)
        out_ref[:, columns] = total.astype(out_ref.dtype)
    for copy in started:
        copy.wait_send()


def dense_mixture(residual, norm_gain, expert_ids, route_weights, w_gate, w_up, w_down):
    local_rows, width = residual.shape
    half = w_gate.shape[3]
    choices = expert_ids.shape[1]
    device_total = lax.axis_size("ep")
    depth = device_total // 4
    groups = [(begin, min(2, depth - begin)) for begin in range(0, depth, 2)]
    parts = 2
    part_width = width // parts
    dma = pltpu.SemaphoreType.DMA
    bf16 = jnp.bfloat16
    vmem = pl.BlockSpec(memory_space=pltpu.VMEM)
    anywhere = pl.BlockSpec(memory_space=pl.ANY)
    flops = 2 * device_total * local_rows * width * half * 6
    return pl.pallas_call(
        functools.partial(mixture_kernel, depth, groups, parts),
        out_shape=jax.ShapeDtypeStruct(residual.shape, residual.dtype),
        in_specs=[anywhere] * 7,
        out_specs=vmem,
        scratch_shapes=[
            pltpu.VMEM((local_rows, width), bf16),
            pltpu.VMEM((width // LANES, LANES), bf16),
            pltpu.VMEM((choices, local_rows), jnp.int32),
            pltpu.VMEM((choices, local_rows), jnp.float32),
            pltpu.VMEM((width, 4 * half), bf16),
            pltpu.VMEM((2 * half, width), bf16),
            pltpu.VMEM((depth, 2, 2, local_rows, width + LANES), bf16),
            pltpu.VMEM((8 * local_rows, 2 * half), bf16),
            pltpu.VMEM((parts, depth, 2, local_rows, part_width), jnp.float32),
            pltpu.VMEM((parts, depth, 2, local_rows, part_width), bf16),
            pltpu.VMEM((parts, depth, 2, local_rows, part_width), bf16),
            pltpu.VMEM((parts, depth, local_rows, part_width), bf16),
            pltpu.VMEM((parts, depth, local_rows, part_width), bf16),
            pltpu.VMEM((parts, depth, local_rows, part_width), bf16),
            pltpu.VMEM((parts, depth, local_rows, part_width), bf16),
            dma((4,)),
            dma((6,)),
            dma((depth, 2, 2)),
            dma((depth,)),
            dma((depth,)),
            dma((depth, 2)),
            dma((len(groups), parts)),
            dma((len(groups), parts)),
            dma((len(groups), parts)),
            dma((len(groups), parts)),
            dma((depth, parts)),
            dma((depth, parts)),
        ],
        compiler_params=pltpu.CompilerParams(
            collective_id=0, has_side_effects=True, vmem_limit_bytes=62 * 2**20
        ),
        cost_estimate=pl.CostEstimate(
            flops=flops, bytes_accessed=12 * width * half, transcendentals=0
        ),
    )(
        residual,
        norm_gain.reshape(width // LANES, LANES),
        expert_ids.T,
        route_weights.T,
        w_gate,
        w_up,
        w_down,
    )


def local(residual, norm_gain, expert_ids, route_weights, w_gate, w_up, w_down):
    local_rows = residual.shape[0]
    model_width = residual.shape[1]
    device_total = lax.axis_size("ep")
    block_total = device_total // 2
    typical = max(1, local_rows * TOP // device_total)
    pair_slots = min(local_rows, 4 * typical)
    if pair_slots == local_rows and device_total % 4 == 0 and device_total <= LANES:
        return dense_mixture(
            residual, norm_gain, expert_ids, route_weights, w_gate, w_up, w_down
        )
    widened = residual.astype(jnp.float32)
    scaling = lax.rsqrt(jnp.mean(widened * widened, axis=1, keepdims=True) + 1e-06)
    normed = (widened * scaling * norm_gain.astype(jnp.float32)[None, :]).astype(jnp.bfloat16)
    shares = (route_weights / jnp.sum(route_weights, axis=1, keepdims=True)).astype(jnp.bfloat16)

    def weighted_both(arrived, arrived_weights):
        flat_rows = arrived.reshape(-1, arrived.shape[2])
        flat_weights = arrived_weights.reshape(-1, 2).astype(jnp.float32)
        mixed = flat_weights[:, 0:1] * half_ffn(flat_rows, w_gate[0, 0], w_up[0, 0], w_down[0, 0])
        mixed = mixed + flat_weights[:, 1:2] * half_ffn(
            flat_rows, w_gate[0, 1], w_up[0, 1], w_down[0, 1]
        )
        return mixed.reshape(arrived.shape)

    half_slots = (pair_slots + 1) // 2
    padded_slots = 2 * half_slots
    picker, slot_rows, slot_weights = pair_tables(
        expert_ids, shares, normed, block_total, padded_slots
    )
    outgoing = slot_rows.reshape(device_total, half_slots, model_width)
    weights_out = slot_weights.reshape(device_total, half_slots, 2)
    arrived = lax.all_to_all(outgoing, "ep", split_axis=0, concat_axis=0, tiled=True)
    arrived_weights = lax.all_to_all(weights_out, "ep", split_axis=0, concat_axis=0, tiled=True)
    other_rows, other_weights = swapped((arrived, arrived_weights), "ep", 0)
    mine = weighted_both(arrived, arrived_weights)
    theirs = weighted_both(other_rows, other_weights)
    back = swapped(theirs, "ep", 0)
    answered = mine + back
    returned = lax.all_to_all(answered, "ep", split_axis=0, concat_axis=0, tiled=True)
    pooled = returned.reshape(block_total * padded_slots, model_width)
    combined = jnp.dot(picker.astype(jnp.float32), pooled, precision=lax.Precision.HIGHEST)
    return (widened + combined).astype(jnp.bfloat16)


def solution(mesh):
    placed = (
        P(("groups", "ep"), None),
        P(),
        P(("groups", "ep"), None),
        P(("groups", "ep"), None),
        P("ep", None, None, None),
        P("ep", None, None, None),
        P("ep", None, None, None),
    )
    return jax.shard_map(
        local, mesh=mesh, in_specs=placed, out_specs=P(("groups", "ep"), None), check_vma=False
    )
```
